512 devices in a mesh: rep: 32 (over z_lo, x), fsdp: 16 (over y, z_hi, core).
Axes of the slice: x: 4, y: 4, z: 16 (z_hi: 2, z_lo: 8; z = z_hi * 8 + z_lo), core: 2. Of those that a mesh axis runs over, the one named last changes fastest.
Arguments:
- hidden_in: bfloat16 [32, 4096, 4096], P('rep', 'fsdp'), may hold values from -6 to 6
- norm_gain: float32 [32, 4096], P('rep'), may hold values from 0.1 to 1.9
- w_value: bfloat16 [32, 4096, 512], P('rep', 'fsdp'), may hold values from -0.09375 to 0.09375
- d_values: bfloat16 [32, 4096, 512], P('rep', 'fsdp'), may hold values from -0.099609375 to 0.099609375
- momentum: float32 [32, 4096, 512], P('rep', 'fsdp'), may hold values from -6 to 6
- step: int32 [], replicated, may hold values from 0 to 63
Outputs:
- values: bfloat16 [32, 4096, 512], P('rep', 'fsdp')
- averaged: float32 [32, 4096, 512], P('rep', 'fsdp')
The draws below stay inside these ranges and needn't reach their ends.
All inputs are finite; a program needn't handle non-finite values.
Results may differ from the reference program's by a relative error of at most 0.0049.
Values may be sent and summed in bfloat16 or wider, within the bound.
A program may use at most 64 MiB of HBM per device.

```python
import jax
import jax.numpy as jnp
from jax import lax

D = 4096
KV = 512
TOKENS = 4096
N_REP = 32


def level_of(rng, dims, shards, smallest, largest):
    factor_of = 1.0
    for position, parts in shards:
        heights = jax.random.uniform(jax.random.fold_in(jax.random.fold_in(rng, 6), position), (parts,), jnp.float32, smallest / len(shards), largest / len(shards))
        factor_of = factor_of * jnp.repeat(jnp.exp(heights), dims[position] // parts).reshape((-1,) + (1,) * (len(dims) - 1 - position))
    return factor_of


def centred(rng, dims, width, most, split=(), kind=jnp.bfloat16):
    level = level_of(rng, dims, split, -0.22, 0.18) if split else 1.0
    drawn = jax.random.normal(rng, dims, jnp.float32) * width * level
    return jnp.minimum(jnp.maximum(drawn, -most), most).astype(kind)


def setup_inputs(seed: int = 0) -> dict:
    streams_of = jax.random.split(jax.random.key(seed), 7)
    hidden_in = centred(streams_of[0], (N_REP, TOKENS, D), 1.0, 6.0, ((0, 32), (1, 16)))
    norm_gain = jnp.clip(1.0 + 0.18 * jax.random.normal(streams_of[1], (N_REP, D), jnp.float32), 0.1, 1.9)
    w_value = centred(streams_of[2], (N_REP, D, KV), D ** -0.5, 0.09375, ((0, 32), (1, 16)))
    d_values = centred(streams_of[3], (N_REP, TOKENS, KV), 0.015625, 0.099609375, ((0, 32), (1, 16)))
    momentum = centred(streams_of[4], (N_REP, D, KV), 1.0, 6.0, ((0, 32), (1, 16)), jnp.float32)
    step = jax.random.randint(streams_of[5], (), 0, 64).astype(jnp.int32)
    return dict(hidden_in=hidden_in, norm_gain=norm_gain, w_value=w_value, d_values=d_values, momentum=momentum, step=step)


def one_replica(items):
    hidden, gain, weight, cotangent, state = items
    rows = hidden.astype(jnp.float32)
    scale = lax.rsqrt(lax.optimization_barrier(jnp.mean(rows * rows, axis=1, keepdims=True)) + 1e-05)
    normed = (rows * scale * gain[None, :]).astype(jnp.bfloat16)
    values = jnp.dot(normed, weight, preferred_element_type=jnp.float32).astype(jnp.bfloat16)
    grad = jnp.dot(normed.T, cotangent, preferred_element_type=jnp.float32)
    updated = 0.9 * state + grad
    return (values, updated)

def reference(hidden_in, norm_gain, w_value, d_values, momentum, step):
    values, updated = lax.map(one_replica, (hidden_in, norm_gain, w_value, d_values, momentum))
    levels = N_REP.bit_length() - 1
    level = (step % levels).astype(jnp.int32)
    partner = jnp.bitwise_xor(jnp.arange(N_REP, dtype=jnp.int32), jnp.left_shift(jnp.int32(1), level))
    averaged = 0.5 * (updated + updated[partner])
    return (values, averaged)
```

```python
from functools import partial

import jax
import jax.numpy as jnp
from jax import lax
from jax.experimental import pallas as pl
from jax.experimental.pallas import tpu as pltpu
from jax.sharding import PartitionSpec as P

MESH = pl.DeviceIdType.MESH
F32 = jnp.float32
BF16 = jnp.bfloat16
N_Y = 4
W_CHUNKS = 4


def kernel(
    level, hid_ref, gain_ref, w_ref, d_ref, mom_ref, values_ref, averaged_ref,
    hid, d_own, mom, normed, to_core, dt, wts, part, vals_in, vals_out,
    g_out, g_in, g_sum, z_out, z_in, x_out, x_in, avg,
    local_sem, send_sem, recv_sem,
):
    rows, feats = hid.shape
    kv = d_own.shape[1]
    blk = w_ref.shape[0]
    rep, shard = lax.axis_index("rep"), lax.axis_index("fsdp")
    core = shard % 2
    half = (shard // 2) % 2
    y = shard // 4

    def at(r, yy, hh, cc):
        return (r, (yy * 2 + hh) * 2 + cc)

    bit = (rep // 2**level) % 2
    pair_rep = rep + (1 - 2 * bit) * 2**level
    y_dev = [None] + [at(rep, (y + k) % N_Y, half, core) for k in range(1, N_Y)]
    z_dev = at(rep, y, 1 - half, core)
    core_dev = at(rep, y, half, 1 - core)
    pair_dev = at(pair_rep, y, half, core)
    cross_dev = z_dev if level < 2 else at(pair_rep, y, 1 - half, core)
    friends = y_dev[1:] + [z_dev, core_dev, pair_dev]
    if level >= 2:
        friends = friends + [cross_dev]

    barrier = pltpu.get_barrier_semaphore()
    for device in friends:
        pl.semaphore_signal(barrier, 1, device_id=device, device_id_type=MESH)

    def fetch(src, dst, i):
        copy = pltpu.make_async_copy(src, dst, local_sem.at[i])
        copy.start()
        return copy

    load_hid = fetch(hid_ref, hid, 0)
    load_d = fetch(d_ref, d_own, 1)
    load_w = fetch(w_ref, wts.at[0], 2)
    load_mom = fetch(mom_ref, mom, 3)

    counter = [0]

    def send(src, dst, device):
        i = counter[0]
        counter[0] += 1
        copy = pltpu.make_async_remote_copy(
            src, dst, send_sem.at[i], recv_sem.at[i], device_id=device, device_id_type=MESH
        )
        copy.start()
        return copy

    load_d.wait()
    dt[0] = d_own[...].astype(F32).T.astype(BF16)
    load_hid.wait()
    step = 32

    def norm_rows(i, carry):
        here = pl.ds(pl.multiple_of(i * step, step), step)
        total = jnp.zeros((step, blk), F32)
        for j in range(feats // blk):
            x = hid[here, j * blk : (j + 1) * blk].astype(F32)
            total = total + x * x
        scale = lax.rsqrt(jnp.sum(total, axis=1, keepdims=True) * (1.0 / feats) + 1e-05)
        for j in range(feats // (2 * blk)):
            for mine in range(2):
                which = core if mine else 1 - core
                cols = pl.ds(pl.multiple_of((2 * j + which) * blk, blk), blk)
                out = (hid[here, cols].astype(F32) * scale * gain_ref[:, cols]).astype(BF16)
                if mine:
                    normed[0, here, j * blk : (j + 1) * blk] = out
                else:
                    to_core[here, j * blk : (j + 1) * blk] = out
        return carry

    lax.fori_loop(0, rows // step, norm_rows, 0)

    pl.semaphore_wait(barrier, len(friends))

    piece = blk // W_CHUNKS
    w_cross = []
    for q in range(W_CHUNKS):
        span = pl.ds(q * piece, piece)
        w_cross.append(send(w_ref.at[span], wts.at[4, span], z_dev))
    core_d = send(dt.at[0], dt.at[1], core_dev)
    core_n = send(to_core, normed.at[1], core_dev)
    w_y = [None] + [send(w_ref, wts.at[N_Y - k], y_dev[k]) for k in range(1, N_Y)]

    def block(k, far):
        hh = 1 - half if far else half
        return pl.multiple_of((((y + k) % N_Y) * 2 + hh) * blk, blk)

    def grad_block(k, far):
        cols = pl.ds(block(k, far), blk)
        return jnp.dot(dt[0], normed[0, :, cols], preferred_element_type=F32) + jnp.dot(
            dt[1], normed[1, :, cols], preferred_element_type=F32
        )

    core_d.wait_recv()
    core_n.wait_recv()
    g_sent = {}
    for far in (1, 0):
        for k in (2, 1, 3):
            slot = far * 3 + k - 1
            g_out[slot] = grad_block(k, far).astype(BF16)
            g_sent[far, k] = send(g_out.at[slot], g_in.at[slot], y_dev[k])
        g_sum[far] = grad_block(0, far)

    def project(k, far, first=False):
        cols = pl.ds(block(k, far), blk)
        for t in range(2):
            new = jnp.dot(normed[t, :, cols], wts[4 * far + k], preferred_element_type=F32)
            part[t] = new if first else part[t] + new

    load_w.wait()
    project(0, 0, True)
    for k in range(1, N_Y):
        w_y[k].wait_recv()
        project(N_Y - k, 0)

    for k in range(1, N_Y):
        g_sent[1, k].wait_recv()
    z_out[...] = (
        g_sum[1] + g_in[3].astype(F32) + g_in[4].astype(F32) + g_in[5].astype(F32)
    ).astype(BF16)
    g_cross = send(z_out, z_in, cross_dev)

    forwards = []
    for q in range(W_CHUNKS):
        span = pl.ds(q * piece, piece)
        w_cross[q].wait_recv()
        for k in range(1, N_Y):
            forwards.append((k, send(wts.at[4, span], wts.at[4 + N_Y - k, span], y_dev[k])))
    project(0, 1)

    for k in range(1, N_Y):
        g_sent[0, k].wait_recv()
    load_mom.wait()
    g_sum[0] = g_sum[0] + g_in[0].astype(F32) + g_in[1].astype(F32) + g_in[2].astype(F32)

    for k in range(1, N_Y):
        for kk, copy in forwards:
            if kk == k:
                copy.wait_recv()
        project(N_Y - k, 1)
    vals_send = send(part.at[1], vals_in, core_dev)
    vals_send.wait_recv()
    vals_out[...] = (part[0] + vals_in[...]).astype(BF16)
    store_vals = fetch(vals_out, values_ref, 4)

    g_cross.wait_recv()
    updated = 0.9 * mom[...] + (g_sum[0] + z_in[...].astype(F32)).T
    avg[...] = updated
    x_out[...] = updated.astype(BF16)
    x_send = send(x_out, x_in, pair_dev)
    x_send.wait_recv()
    avg[...] = 0.5 * (avg[...] + x_in[...].astype(F32))
    store_avg = fetch(avg, averaged_ref, 5)

    for copy in w_cross + w_y[1:] + [core_d, core_n, g_cross, vals_send, x_send]:
        copy.wait_send()
    for copy in g_sent.values():
        copy.wait_send()
    for _, copy in forwards:
        copy.wait_send()
    store_vals.wait()
    store_avg.wait()


def fused(level, hidden, gain, weight, cotangent, momentum):
    rows, feats = hidden.shape
    blk, kv = weight.shape
    copies = W_CHUNKS * N_Y + 2 + 3 + 6 + 1 + 1 + 1
    anywhere = pl.BlockSpec(memory_space=pl.ANY)
    return pl.pallas_call(
        partial(kernel, level),
        name=f"layer_level_{level}",
        out_shape=(
            jax.ShapeDtypeStruct((rows, kv), BF16),
            jax.ShapeDtypeStruct((blk, kv), F32),
        ),
        in_specs=[
            anywhere,
            pl.BlockSpec(memory_space=pltpu.VMEM),
            anywhere,
            anywhere,
            anywhere,
        ],
        out_specs=(anywhere, anywhere),
        scratch_shapes=[
            pltpu.VMEM((rows, feats), BF16),
            pltpu.VMEM((rows, kv), BF16),
            pltpu.VMEM((blk, kv), F32),
            pltpu.VMEM((2, rows, feats // 2), BF16),
            pltpu.VMEM((rows, feats // 2), BF16),
            pltpu.VMEM((2, kv, rows), BF16),
            pltpu.VMEM((8, blk, kv), BF16),
            pltpu.VMEM((2, rows, kv), F32),
            pltpu.VMEM((rows, kv), F32),
            pltpu.VMEM((rows, kv), BF16),
            pltpu.VMEM((6, kv, blk), BF16),
            pltpu.VMEM((6, kv, blk), BF16),
            pltpu.VMEM((2, kv, blk), F32),
            pltpu.VMEM((kv, blk), BF16),
            pltpu.VMEM((kv, blk), BF16),
            pltpu.VMEM((blk, kv), BF16),
            pltpu.VMEM((blk, kv), BF16),
            pltpu.VMEM((blk, kv), F32),
            pltpu.SemaphoreType.DMA((6,)),
            pltpu.SemaphoreType.DMA((copies,)),
            pltpu.SemaphoreType.DMA((copies,)),
        ],
        compiler_params=pltpu.CompilerParams(
            collective_id=level, has_side_effects=True, vmem_limit_bytes=40 << 20
        ),
    )(hidden, gain, weight, cotangent, momentum)


def local(hidden_in, norm_gain, w_value, d_values, momentum, step):
    levels = lax.axis_size("rep").bit_length() - 1
    branches = [partial(fused, level) for level in range(levels)]
    values, averaged = lax.switch(
        step % levels, branches, hidden_in[0], norm_gain, w_value[0], d_values[0], momentum[0]
    )
    return (values[None], averaged[None])


def solution(mesh):
    placed = (
        P("rep", "fsdp", None),
        P("rep", None),
        P("rep", "fsdp", None),
        P("rep", "fsdp", None),
        P("rep", "fsdp", None),
        P(),
    )
    return jax.shard_map(
        local,
        mesh=mesh,
        in_specs=placed,
        out_specs=(P("rep", "fsdp", None), P("rep", "fsdp", None)),
        check_vma=False,
    )
```

```python
from functools import partial

import jax
import jax.numpy as jnp
from jax import lax
from jax.experimental import pallas as pl
from jax.experimental.pallas import tpu as pltpu
from jax.sharding import PartitionSpec as P

MESH = pl.DeviceIdType.MESH
F32 = jnp.float32
BF16 = jnp.bfloat16
N_X = 4
N_Y = 4
X_LEVELS = 2
W_CHUNKS = 4
BACK = 2


def copies_of(level):
    common = W_CHUNKS + 4 + 6 + 3 * W_CHUNKS + BACK
    return common + (22 + BACK if level < X_LEVELS else 12 + 3 * BACK)


def kernel(
    level, hid_ref, gain_ref, w_ref, d_ref, mom_ref, values_ref, averaged_ref,
    hid, mom, normed, to_core, d, wts, part, vals_in,
    keep, keep_side, first_out, first_in, side_out, side_in, own_out, own_in,
    z_out, z_in, back_out, back_in,
    local_sem, send_sem, recv_sem,
):
    along_x = level < X_LEVELS
    rows, feats = hid.shape
    blk, kv = w_ref.shape
    mid, cols = blk // 2, kv // 2
    rep, shard = lax.axis_index("rep"), lax.axis_index("fsdp")
    y, half, core = shard // 4, (shard // 2) % 2, shard % 2

    def at(r, yy, hh, cc):
        return (r, (((yy + N_Y) % N_Y) * 2 + hh) * 2 + cc)

    bit = (rep // 2**level) % 2
    pair_rep = rep + (1 - 2 * bit) * 2**level
    up, down = at(rep, y + 1, half, core), at(rep, y - 1, half, core)
    across = at(rep, y, 1 - half, core)
    other = at(rep, y, half, 1 - core)
    pair = at(pair_rep, y, half, core)
    friends = [up, down, across, other, pair]
    if along_x:
        pair_up, pair_down = at(pair_rep, y + 1, half, core), at(pair_rep, y - 1, half, core)
        friends = friends + [pair_up, pair_down]
    else:
        pair_across = at(pair_rep, y, 1 - half, core)
        friends = friends + [pair_across]

    barrier = pltpu.get_barrier_semaphore()
    for device in friends:
        pl.semaphore_signal(barrier, 1, device_id=device, device_id_type=MESH)

    def fetch(src, dst, i):
        copy = pltpu.make_async_copy(src, dst, local_sem.at[i])
        copy.start()
        return copy

    load_hid = fetch(hid_ref, hid, 0)
    load_d = fetch(d_ref, d.at[0], 1)

    sent = []

    def send(src, dst, device):
        i = len(sent)
        copy = pltpu.make_async_remote_copy(
            src, dst, send_sem.at[i], recv_sem.at[i], device_id=device, device_id_type=MESH
        )
        copy.start()
        sent.append(copy)
        return copy

    pl.semaphore_wait(barrier, len(friends))

    def piece(q):
        n = blk // W_CHUNKS
        return pl.ds(q * n, n)

    w_cross = [send(w_ref.at[piece(q)], wts.at[4, piece(q)], across) for q in range(W_CHUNKS)]
    load_w = fetch(w_ref, wts.at[0], 2)
    load_mom = fetch(mom_ref, mom, 3)
    load_d.wait()
    core_d = send(d.at[0], d.at[1], other)

    step = 32

    def norm_rows(i, carry):
        here = pl.ds(pl.multiple_of(i * step, step), step)
        total = jnp.zeros((step, blk), F32)
        for j in range(feats // blk):
            v = hid[here, j * blk : (j + 1) * blk].astype(F32)
            total = total + v * v
        scale = lax.rsqrt(jnp.sum(total, axis=1, keepdims=True) * (1.0 / feats) + 1e-05)
        for j in range(2 * N_Y):
            for mine in range(2):
                which = core if mine else 1 - core
                span = pl.ds(pl.multiple_of((2 * j + which) * blk, blk), blk)
                out = (hid[here, span].astype(F32) * scale * gain_ref[:, span]).astype(BF16)
                if mine:
                    normed[0, j % 2, j // 2, here] = out
                else:
                    to_core[j % 2, j // 2, here] = out
        return carry

    load_hid.wait()
    lax.fori_loop(0, rows // step, norm_rows, 0)
    core_n = {
        1: send(to_core.at[1 - half], normed.at[1, 1 - half], other),
        0: send(to_core.at[half], normed.at[1, half], other),
    }

    def tokens_of(t, k, far):
        return normed[t, 1 - half if far else half, (y + k) % N_Y]

    def grad_block(k, far):
        return sum(
            lax.dot_general(
                tokens_of(t, k, far), d[t], (((0,), (0,)), ((), ())), preferred_element_type=F32
            )
            for t in range(2)
        )

    mine = pl.ds(pl.multiple_of(bit * mid, mid), mid)
    theirs = pl.ds(pl.multiple_of((1 - bit) * mid, mid), mid)
    first, side, own = {}, {0: [], 1: []}, {}

    def send_side(far, way, part_of):
        src = side_out.at[far, way, part_of]
        if along_x:
            ends = ((up, down)[way], (pair_up, pair_down)[way])
            for i, span in enumerate((mine, theirs)):
                side[far].append(
                    send(src.at[span], side_in.at[far, way, part_of, pl.ds(i * mid, mid)], ends[i])
                )
        else:
            side[far].append(send(src, side_in.at[far, way, part_of], (up, down)[way]))

    def reduce_first(far):
        block = grad_block(2, far).astype(BF16)
        first_out[far, 0] = block[:, :cols]
        first_out[far, 1] = block[:, cols:]
        first[far] = [
            send(first_out.at[far, 0], first_in.at[far, 0], up),
            send(first_out.at[far, 1], first_in.at[far, 1], down),
        ]
        for way, k in ((0, 1), (1, 3)):
            block = grad_block(k, far)
            parts = (block[:, :cols], block[:, cols:])
            side_out[far, way, 1 - way] = parts[1 - way].astype(BF16)
            send_side(far, way, 1 - way)
            keep_side[far, way] = parts[way]
        block = grad_block(0, far)
        if not far:
            block = block + 0.9 * mom[...]
        keep[far] = block
        if along_x:
            own_out[far] = keep[far, theirs].astype(BF16)
            own[far] = send(own_out.at[far], own_in.at[far], pair)

    def reduce_second(far):
        for way in range(2):
            first[far][way].wait_recv()
            side_out[far, way, way] = (
                keep_side[far, way] + first_in[far, way].astype(F32)
            ).astype(BF16)
            send_side(far, way, way)

    def reduced(far, span, copies):
        total = keep[far, span]
        for at_row in copies:
            for way in range(2):
                total = total + jnp.concatenate(
                    [side_in[far, way, c, pl.ds(at_row, mid)] for c in range(2)], axis=1
                ).astype(F32)
        return total

    def wait_reduced(far):
        for copy in side[far]:
            copy.wait_recv()
        if along_x:
            own[far].wait_recv()

    def project(k, far, begin=False, tokens=(0, 1)):
        for t in tokens:
            new = jnp.dot(tokens_of(t, k, far), wts[4 * far + k], preferred_element_type=F32)
            part[t] = new if begin else part[t] + new

    def back_rows(i):
        n = mid // BACK
        return pl.ds(i * n, n)

    core_d.wait_recv()
    core_n[1].wait_recv()
    reduce_first(1)
    core_n[0].wait_recv()
    load_w.wait()
    load_mom.wait()
    project(0, 0, True)
    reduce_second(1)
    reduce_first(0)

    wait_reduced(1)
    crossing = []
    if along_x:
        z_out[0] = (reduced(1, mine, (0, mid)) + own_in[1].astype(F32)).astype(BF16)
        for i in range(BACK):
            crossing.append(send(z_out.at[0, back_rows(i)], z_in.at[0, back_rows(i)], across))
    else:
        for i, span in enumerate((mine, theirs)):
            start = bit * mid if i == 0 else (1 - bit) * mid
            z_out[i] = reduced(1, span, (pl.multiple_of(start, mid),)).astype(BF16)
        for q in range(BACK):
            for i, device in enumerate((across, pair_across)):
                crossing.append(send(z_out.at[i, back_rows(q)], z_in.at[i, back_rows(q)], device))

    far_up, far_down, far_relay = {}, {}, []

    def spread(q):
        w_cross[q].wait_recv()
        s = piece(q)
        for way in (q % 2, 1 - q % 2):
            if way == 0:
                far_up[q] = send(wts.at[4, s], wts.at[7, s], up)
            else:
                far_down[q] = send(wts.at[4, s], wts.at[5, s], down)

    def relay(q):
        s = piece(q)
        if q % 2 == 0:
            far_up[q].wait_recv()
            far_relay.append(send(wts.at[7, s], wts.at[6, s], up))
        else:
            far_down[q].wait_recv()
            far_relay.append(send(wts.at[5, s], wts.at[6, s], down))

    spread(0)
    reduce_second(0)
    lower, upper = pl.ds(0, mid), pl.ds(mid, mid)
    near_up = [send(w_ref.at[s], wts.at[3, s], up) for s in (lower, upper)]
    near_down = [send(w_ref.at[s], wts.at[1, s], down) for s in (upper, lower)]
    spread(1)
    relay(0)
    wait_reduced(0)
    pair_near = []
    if along_x:
        keep[0, mine] = reduced(0, mine, (0, mid)) + own_in[0].astype(F32)
    else:
        z_out[2] = reduced(0, theirs, (pl.multiple_of((1 - bit) * mid, mid),)).astype(BF16)
        for q in range(BACK):
            pair_near.append(send(z_out.at[2, back_rows(q)], z_in.at[2, back_rows(q)], pair))
        keep[0, mine] = reduced(0, mine, (pl.multiple_of(bit * mid, mid),))
    near_up[0].wait_recv()
    near_down[0].wait_recv()
    near_relay = [
        send(wts.at[3, lower], wts.at[2, lower], up),
        send(wts.at[1, upper], wts.at[2, upper], down),
    ]
    spread(2)
    relay(1)
    near_up[1].wait_recv()
    near_down[1].wait_recv()
    project(1, 0)
    project(3, 0)
    spread(3)
    relay(2)
    project(0, 1)
    relay(3)
    for copy in near_relay:
        copy.wait_recv()
    project(2, 0)
    for q in range(W_CHUNKS):
        if q % 2 == 0:
            far_down[q].wait_recv()
        else:
            far_up[q].wait_recv()
    project(1, 1)
    project(3, 1)

    back = []

    def finish(q):
        s = back_rows(q)
        n = mid // BACK
        total = keep[0, pl.ds(pl.multiple_of(bit * mid + q * n, n), n)]
        if along_x:
            crossing[q].wait_recv()
            total = total + z_in[0, s].astype(F32)
        else:
            crossing[2 * q].wait_recv()
            crossing[2 * q + 1].wait_recv()
            pair_near[q].wait_recv()
            total = total + z_in[0, s].astype(F32) + z_in[1, s].astype(F32) + z_in[2, s].astype(F32)
        result = 0.5 * total
        back_out[s] = result.astype(BF16)
        back.append(send(back_out.at[s], back_in.at[s], pair))
        averaged_ref[pl.ds(pl.multiple_of(bit * mid + q * n, n), n)] = result

    for copy in far_relay:
        copy.wait_recv()
    project(2, 1, tokens=(1,))
    vals_send = send(part.at[1], vals_in, other)
    project(2, 1, tokens=(0,))
    for q in range(BACK):
        finish(q)
    vals_send.wait_recv()
    values_ref[...] = (part[0] + vals_in[...]).astype(BF16)
    for copy in back:
        copy.wait_recv()
    averaged_ref[theirs] = back_in[...].astype(F32)

    assert len(sent) == copies_of(level)
    for copy in sent:
        copy.wait_send()


def fused(level, hidden, gain, weight, cotangent, momentum):
    rows, feats = hidden.shape
    blk, kv = weight.shape
    mid, cols = blk // 2, kv // 2
    anywhere = pl.BlockSpec(memory_space=pl.ANY)
    vmem = pl.BlockSpec(memory_space=pltpu.VMEM)
    return pl.pallas_call(
        partial(kernel, level),
        name=f"layer_level_{level}",
        out_shape=(
            jax.ShapeDtypeStruct((rows, kv), BF16),
            jax.ShapeDtypeStruct((blk, kv), F32),
        ),
        in_specs=[anywhere, vmem, anywhere, anywhere, anywhere],
        out_specs=(vmem, vmem),
        scratch_shapes=[
            pltpu.VMEM((rows, feats), BF16),
            pltpu.VMEM((blk, kv), F32),
            pltpu.VMEM((2, 2, N_Y, rows, blk), BF16),
            pltpu.VMEM((2, N_Y, rows, blk), BF16),
            pltpu.VMEM((2, rows, kv), BF16),
            pltpu.VMEM((2 * N_Y, blk, kv), BF16),
            pltpu.VMEM((2, rows, kv), F32),
            pltpu.VMEM((rows, kv), F32),
            pltpu.VMEM((2, blk, kv), F32),
            pltpu.VMEM((2, 2, blk, cols), F32),
            pltpu.VMEM((2, 2, blk, cols), BF16),
            pltpu.VMEM((2, 2, blk, cols), BF16),
            pltpu.VMEM((2, 2, 2, blk, cols), BF16),
            pltpu.VMEM((2, 2, 2, blk, cols), BF16),
            pltpu.VMEM((2, mid, kv), BF16),
            pltpu.VMEM((2, mid, kv), BF16),
            pltpu.VMEM((3, mid, kv), BF16),
            pltpu.VMEM((3, mid, kv), BF16),
            pltpu.VMEM((mid, kv), BF16),
            pltpu.VMEM((mid, kv), BF16),
            pltpu.SemaphoreType.DMA((4,)),
            pltpu.SemaphoreType.DMA((copies_of(level),)),
            pltpu.SemaphoreType.DMA((copies_of(level),)),
        ],
        compiler_params=pltpu.CompilerParams(
            collective_id=level, has_side_effects=True, vmem_limit_bytes=40 << 20
        ),
    )(hidden, gain, weight, cotangent, momentum)


def local(hidden_in, norm_gain, w_value, d_values, momentum, step):
    levels = lax.axis_size("rep").bit_length() - 1
    branches = [partial(fused, level) for level in range(levels)]
    values, averaged = lax.switch(
        step % levels, branches, hidden_in[0], norm_gain, w_value[0], d_values[0], momentum[0]
    )
    return (values[None], averaged[None])


def solution(mesh):
    placed = (
        P("rep", "fsdp", None),
        P("rep", None),
        P("rep", "fsdp", None),
        P("rep", "fsdp", None),
        P("rep", "fsdp", None),
        P(),
    )
    return jax.shard_map(
        local,
        mesh=mesh,
        in_specs=placed,
        out_specs=(P("rep", "fsdp", None), P("rep", "fsdp", None)),
        check_vma=False,
    )
```

```python
from functools import partial

import jax
import jax.numpy as jnp
from jax import lax
from jax.experimental import pallas as pl
from jax.experimental.pallas import tpu as pltpu
from jax.sharding import PartitionSpec as P

MESH = pl.DeviceIdType.MESH
F32 = jnp.float32
BF16 = jnp.bfloat16
N_X = 4
N_Y = 4
X_LEVELS = 2
W_CHUNKS = 4
STORE = True
BACK = 2
EARLY = 4
N_SEND, N_RECV = 13, 32


def kernel(
    level, hid_ref, gain_ref, w_ref, d_ref, mom_ref, values_ref, averaged_ref,
    hid, mom, normed, to_core, d, wts, part, vals_in,
    keep, keep_side, first_out, first_in, side_out, side_in, own_out, own_in,
    z_out, z_in, back_out, back_in,
    local_sem, send_sem, recv_sem, ready,
):
    along_x = level < X_LEVELS
    rows, feats = hid.shape
    blk, kv = w_ref.shape
    mid, cols = blk // 2, kv // 2
    rep, shard = lax.axis_index("rep"), lax.axis_index("fsdp")
    y, half, core = shard // 4, (shard // 2) % 2, shard % 2

    def at(r, yy, hh, cc):
        return (r, (((yy + N_Y) % N_Y) * 2 + hh) * 2 + cc)

    bit = (rep // 2**level) % 2
    pair_rep = rep + (1 - 2 * bit) * 2**level
    up, down = at(rep, y + 1, half, core), at(rep, y - 1, half, core)
    across = at(rep, y, 1 - half, core)
    other = at(rep, y, half, 1 - core)
    pair = at(pair_rep, y, half, core)
    friends, far_friends = [up, down, other, pair], [across]
    if along_x:
        pair_up, pair_down = at(pair_rep, y + 1, half, core), at(pair_rep, y - 1, half, core)
        friends = friends + [pair_up, pair_down]
    else:
        pair_across = at(pair_rep, y, 1 - half, core)
        far_friends = far_friends + [pair_across]

    def signal(semaphore, devices):
        for device in devices:
            pl.semaphore_signal(semaphore, 1, device_id=device, device_id_type=MESH)

    barrier = pltpu.get_barrier_semaphore()
    if along_x:
        ahead = rep // N_X < EARLY
        knows = jnp.logical_or(half == 1, jnp.logical_not(ahead))
        pl.when(jnp.logical_or(half == 0, jnp.logical_not(ahead)))(
            lambda: signal(barrier, far_friends)
        )
    else:
        signal(barrier, far_friends)
    signal(barrier, friends)

    def fetch(src, dst, i):
        copy = pltpu.make_async_copy(src, dst, local_sem.at[i])
        copy.start()
        return copy

    load_hid = fetch(hid_ref, hid, 0)
    load_d = fetch(d_ref, d.at[0], 1)

    leaving, landing = {}, {}

    def send(src, dst, device, leave, land, start=True):
        copy = pltpu.make_async_remote_copy(
            src,
            dst,
            send_sem.at[leaving.setdefault(leave, len(leaving))],
            recv_sem.at[landing.setdefault(land, len(landing))],
            device_id=device,
            device_id_type=MESH,
        )
        if start:
            copy.start()
        return copy

    def landed(land, whole):
        pltpu.make_async_copy(whole, whole, recv_sem.at[landing[land]]).wait()

    if along_x:
        pl.semaphore_wait(barrier, len(friends) + knows.astype(jnp.int32) * len(far_friends))
        pl.when(jnp.logical_and(half == 1, ahead))(lambda: signal(ready, far_friends))
    else:
        pl.semaphore_wait(barrier, len(friends) + len(far_friends))

    def piece(q):
        n = blk // W_CHUNKS
        return pl.ds(q * n, n)

    w_cross = [
        send(w_ref.at[piece(q)], wts.at[4, piece(q)], across, "w", f"w{q}", start=False)
        for q in range(W_CHUNKS)
    ]

    def start_w():
        for copy in w_cross:
            copy.start()

    if along_x:
        pl.when(knows)(start_w)
    else:
        start_w()
    load_w = fetch(w_ref, wts.at[0], 2)
    load_mom = fetch(mom_ref, mom, 3)
    load_d.wait()
    core_d = send(d.at[0], d.at[1], other, "d", "d")

    step = 32

    def norm_rows(i, carry):
        here = pl.ds(pl.multiple_of(i * step, step), step)
        total = jnp.zeros((step, blk), F32)
        for j in range(feats // blk):
            v = hid[here, j * blk : (j + 1) * blk].astype(F32)
            total = total + v * v
        scale = lax.rsqrt(jnp.sum(total, axis=1, keepdims=True) * (1.0 / feats) + 1e-05)
        for j in range(2 * N_Y):
            for mine in range(2):
                which = core if mine else 1 - core
                span = pl.ds(pl.multiple_of((2 * j + which) * blk, blk), blk)
                out = (hid[here, span].astype(F32) * scale * gain_ref[:, span]).astype(BF16)
                if mine:
                    normed[0, j % 2, j // 2, here] = out
                else:
                    to_core[j % 2, j // 2, here] = out
        return carry

    load_hid.wait()
    lax.fori_loop(0, rows // step, norm_rows, 0)
    core_n = {
        1: send(to_core.at[1 - half], normed.at[1, 1 - half], other, "n", "n1"),
        0: send(to_core.at[half], normed.at[1, half], other, "n", "n0"),
    }

    def tokens_of(t, k, far):
        return normed[t, 1 - half if far else half, (y + k) % N_Y]

    def grad_block(k, far):
        return sum(
            lax.dot_general(
                tokens_of(t, k, far), d[t], (((0,), (0,)), ((), ())), preferred_element_type=F32
            )
            for t in range(2)
        )

    mine = pl.ds(pl.multiple_of(bit * mid, mid), mid)
    theirs = pl.ds(pl.multiple_of((1 - bit) * mid, mid), mid)
    first, own = {}, {}

    def send_side(far, way, part_of):
        src = side_out.at[far, way, part_of]
        if along_x:
            ends = ((up, down)[way], (pair_up, pair_down)[way])
            for i, span in enumerate((mine, theirs)):
                dst = side_in.at[far, way, part_of, pl.ds(i * mid, mid)]
                send(src.at[span], dst, ends[i], "side", f"side{far}")
        else:
            send(src, side_in.at[far, way, part_of], (up, down)[way], "side", f"side{far}")

    def reduce_first(far):
        block = grad_block(2, far).astype(BF16)
        first_out[far, 0] = block[:, :cols]
        first_out[far, 1] = block[:, cols:]
        first[far] = [
            send(first_out.at[far, 0], first_in.at[far, 0], up, "first", f"first{far}0"),
            send(first_out.at[far, 1], first_in.at[far, 1], down, "first", f"first{far}1"),
        ]
        for way, k in ((0, 1), (1, 3)):
            block = grad_block(k, far)
            parts = (block[:, :cols], block[:, cols:])
            side_out[far, way, 1 - way] = parts[1 - way].astype(BF16)
            send_side(far, way, 1 - way)
            keep_side[far, way] = parts[way]
        block = grad_block(0, far)
        if not far:
            block = block + 0.9 * mom[...]
        keep[far] = block
        if along_x:
            own_out[far] = keep[far, theirs].astype(BF16)
            own[far] = send(own_out.at[far], own_in.at[far], pair, "own", f"own{far}")

    def reduce_second(far):
        for way in range(2):
            first[far][way].wait_recv()
            side_out[far, way, way] = (
                keep_side[far, way] + first_in[far, way].astype(F32)
            ).astype(BF16)
            send_side(far, way, way)

    def reduced(far, span, copies):
        total = keep[far, span]
        for at_row in copies:
            for way in range(2):
                total = total + jnp.concatenate(
                    [side_in[far, way, c, pl.ds(at_row, mid)] for c in range(2)], axis=1
                ).astype(F32)
        return total

    def wait_reduced(far):
        landed(f"side{far}", side_in.at[far])
        if along_x:
            own[far].wait_recv()

    def project(k, far, begin=False, tokens=(0, 1)):
        for t in tokens:
            new = jnp.dot(tokens_of(t, k, far), wts[4 * far + k], preferred_element_type=F32)
            part[t] = new if begin else part[t] + new

    def back_rows(i):
        n = mid // BACK
        return pl.ds(i * n, n)

    core_d.wait_recv()
    core_n[1].wait_recv()
    reduce_first(1)
    core_n[0].wait_recv()
    load_w.wait()
    load_mom.wait()
    project(0, 0, True)
    reduce_second(1)
    reduce_first(0)


    def start_lower():
        pl.semaphore_wait(ready, len(far_friends))
        start_w()

    if along_x:
        pl.when(jnp.logical_not(knows))(start_lower)
    wait_reduced(1)
    if along_x:
        z_out[0] = (reduced(1, mine, (0, mid)) + own_in[1].astype(F32)).astype(BF16)
        for i in range(BACK):
            send(z_out.at[0, back_rows(i)], z_in.at[0, back_rows(i)], across, "z", f"z{i}")
    else:
        for i, span in enumerate((mine, theirs)):
            start = bit * mid if i == 0 else (1 - bit) * mid
            z_out[i] = reduced(1, span, (pl.multiple_of(start, mid),)).astype(BF16)
        for q in range(BACK):
            for i, device in enumerate((across, pair_across)):
                send(z_out.at[i, back_rows(q)], z_in.at[i, back_rows(q)], device, "z", f"z{q}")

    far_up, far_down = {}, {}

    def spread(q):
        w_cross[q].wait_recv()
        s = piece(q)
        for way in (q % 2, 1 - q % 2):
            if way == 0:
                land = f"far{q}" if q % 2 == 0 else "far"
                far_up[q] = send(wts.at[4, s], wts.at[7, s], up, "far", land)
            else:
                land = f"far{q}" if q % 2 else "far"
                far_down[q] = send(wts.at[4, s], wts.at[5, s], down, "far", land)

    def relay(q):
        s = piece(q)
        if q % 2 == 0:
            far_up[q].wait_recv()
            send(wts.at[7, s], wts.at[6, s], up, "far_relay", "far_relay")
        else:
            far_down[q].wait_recv()
            send(wts.at[5, s], wts.at[6, s], down, "far_relay", "far_relay")

    spread(0)
    reduce_second(0)
    lower, upper = pl.ds(0, mid), pl.ds(mid, mid)
    for i, (s_up, s_down) in enumerate(((lower, upper), (upper, lower))):
        send(w_ref.at[s_up], wts.at[3, s_up], up, "near", f"near{i}")
        send(w_ref.at[s_down], wts.at[1, s_down], down, "near", f"near{i}")
    spread(1)
    relay(0)
    wait_reduced(0)
    if along_x:
        keep[0, mine] = reduced(0, mine, (0, mid)) + own_in[0].astype(F32)
    else:
        z_out[2] = reduced(0, theirs, (pl.multiple_of((1 - bit) * mid, mid),)).astype(BF16)
        for q in range(BACK):
            send(z_out.at[2, back_rows(q)], z_in.at[2, back_rows(q)], pair, "z", f"z{q}")
        keep[0, mine] = reduced(0, mine, (pl.multiple_of(bit * mid, mid),))
    landed("near0", wts.at[1])
    send(wts.at[3, lower], wts.at[2, lower], up, "near_relay", "near_relay")
    send(wts.at[1, upper], wts.at[2, upper], down, "near_relay", "near_relay")
    spread(2)
    relay(1)
    landed("near1", wts.at[1])
    project(1, 0)
    project(3, 0)
    spread(3)
    relay(2)
    project(0, 1)
    relay(3)
    landed("near_relay", wts.at[2])
    project(2, 0)
    landed("far", wts.at[5])
    project(1, 1)
    project(3, 1)

    def finish(q):
        s = back_rows(q)
        n = mid // BACK
        total = keep[0, pl.ds(pl.multiple_of(bit * mid + q * n, n), n)]
        if along_x:
            landed(f"z{q}", z_in.at[0, s])
            total = total + z_in[0, s].astype(F32)
        else:
            landed(f"z{q}", z_in.at[:, s])
            total = total + z_in[0, s].astype(F32) + z_in[1, s].astype(F32) + z_in[2, s].astype(F32)
        result = 0.5 * total
        back_out[s] = result.astype(BF16)
        send(back_out.at[s], back_in.at[s], pair, "back", "back")
        averaged_ref[pl.ds(pl.multiple_of(bit * mid + q * n, n), n)] = result

    landed("far_relay", wts.at[6])
    project(2, 1, tokens=(1,))
    vals_send = send(part.at[1], vals_in, other, "vals", "vals")
    project(2, 1, tokens=(0,))
    for q in range(BACK):
        finish(q)
    vals_send.wait_recv()
    values_ref[...] = (part[0] + vals_in[...]).astype(BF16)
    landed("back", back_in)
    averaged_ref[theirs] = back_in[...].astype(F32)

    total_of = {
        "w": wts.at[4],
        "d": d.at[0],
        "n": to_core,
        "first": first_out,
        "side": side_out,
        "own": own_out,
        "z": z_out.at[0] if along_x else z_out,
        "far": wts.at[pl.ds(4, 2)],
        "far_relay": wts.at[6],
        "near": wts.at[pl.ds(0, 2)],
        "near_relay": wts.at[2],
        "vals": vals_in,
        "back": back_in,
    }
    assert len(leaving) <= N_SEND and len(landing) <= N_RECV
    for leave, i in leaving.items():
        pltpu.make_async_copy(total_of[leave], total_of[leave], send_sem.at[i]).wait()


def fused(level, hidden, gain, weight, cotangent, momentum):
    rows, feats = hidden.shape
    blk, kv = weight.shape
    mid, cols = blk // 2, kv // 2
    anywhere = pl.BlockSpec(memory_space=pl.ANY)
    vmem = pl.BlockSpec(memory_space=pltpu.VMEM)
    return pl.pallas_call(
        partial(kernel, level),
        name=f"layer_level_{level}",
        out_shape=(
            jax.ShapeDtypeStruct((rows, kv), BF16),
            jax.ShapeDtypeStruct((blk, kv), F32),
        ),
        in_specs=[anywhere, vmem, anywhere, anywhere, anywhere],
        out_specs=(vmem, vmem),
        scratch_shapes=[
            pltpu.VMEM((rows, feats), BF16),
            pltpu.VMEM((blk, kv), F32),
            pltpu.VMEM((2, 2, N_Y, rows, blk), BF16),
            pltpu.VMEM((2, N_Y, rows, blk), BF16),
            pltpu.VMEM((2, rows, kv), BF16),
            pltpu.VMEM((2 * N_Y, blk, kv), BF16),
            pltpu.VMEM((2, rows, kv), F32),
            pltpu.VMEM((rows, kv), F32),
            pltpu.VMEM((2, blk, kv), F32),
            pltpu.VMEM((2, 2, blk, cols), F32),
            pltpu.VMEM((2, 2, blk, cols), BF16),
            pltpu.VMEM((2, 2, blk, cols), BF16),
            pltpu.VMEM((2, 2, 2, blk, cols), BF16),
            pltpu.VMEM((2, 2, 2, blk, cols), BF16),
            pltpu.VMEM((2, mid, kv), BF16),
            pltpu.VMEM((2, mid, kv), BF16),
            pltpu.VMEM((3, mid, kv), BF16),
            pltpu.VMEM((3, mid, kv), BF16),
            pltpu.VMEM((mid, kv), BF16),
            pltpu.VMEM((mid, kv), BF16),
            pltpu.SemaphoreType.DMA((4,)),
            pltpu.SemaphoreType.DMA((N_SEND,)),
            pltpu.SemaphoreType.DMA((N_RECV,)),
            pltpu.SemaphoreType.REGULAR,
        ],
        compiler_params=pltpu.CompilerParams(
            collective_id=level, has_side_effects=True, vmem_limit_bytes=40 << 20
        ),
    )(hidden, gain, weight, cotangent, momentum)


def store_kernel(values_ref, averaged_ref, values_out, averaged_out, sems):
    copies = [
        pltpu.make_async_copy(values_ref, values_out, sems.at[0]),
        pltpu.make_async_copy(averaged_ref, averaged_out, sems.at[1]),
    ]
    for copy in copies:
        copy.start()
    for copy in copies:
        copy.wait()


def store(values, averaged):
    anywhere = pl.BlockSpec(memory_space=pl.ANY)
    return pl.pallas_call(
        store_kernel,
        name="store",
        out_shape=(
            jax.ShapeDtypeStruct(values.shape, values.dtype),
            jax.ShapeDtypeStruct(averaged.shape, averaged.dtype),
        ),
        in_specs=[anywhere, anywhere],
        out_specs=(anywhere, anywhere),
        scratch_shapes=[pltpu.SemaphoreType.DMA((2,))],
    )(values, averaged)


def local(hidden_in, norm_gain, w_value, d_values, momentum, step):
    levels = lax.axis_size("rep").bit_length() - 1
    branches = [partial(fused, level) for level in range(levels)]
    values, averaged = lax.switch(
        lax.rem(step, levels), branches, hidden_in[0], norm_gain, w_value[0], d_values[0], momentum[0]
    )
    if STORE:
        values, averaged = store(values, averaged)
    return (values[None], averaged[None])


def solution(mesh):
    placed = (
        P("rep", "fsdp", None),
        P("rep", None),
        P("rep", "fsdp", None),
        P("rep", "fsdp", None),
        P("rep", "fsdp", None),
        P(),
    )
    return jax.shard_map(
        local,
        mesh=mesh,
        in_specs=placed,
        out_specs=(P("rep", "fsdp", None), P("rep", "fsdp", None)),
        check_vma=False,
    )
```

```python
from functools import partial

import jax
import jax.numpy as jnp
from jax import lax
from jax.experimental import pallas as pl
from jax.experimental.pallas import tpu as pltpu
from jax.sharding import PartitionSpec as P

MESH = pl.DeviceIdType.MESH
F32 = jnp.float32
BF16 = jnp.bfloat16
N_X = 4
N_Y = 4
X_LEVELS = 2
W_CHUNKS = 4
BACK = 2
EARLY = 4
N_SEND, N_RECV = 13, 32


def kernel(
    level, hid_ref, gain_ref, w_ref, d_ref, mom_ref, values_ref, averaged_ref,
    hid, mom, normed, to_core, d, wts, part, vals_in,
    keep, keep_side, first_out, first_in, side_out, side_in, own_out, own_in,
    z_out, z_in, back_out, back_in,
    local_sem, send_sem, recv_sem, ready,
):
    along_x = level < X_LEVELS
    ahead_of = EARLY if along_x or 2**level < EARLY * N_X else 0
    rows, feats = hid.shape
    blk, kv = w_ref.shape
    mid, cols = blk // 2, kv // 2
    rep, shard = lax.axis_index("rep"), lax.axis_index("fsdp")
    y, half, core = shard // 4, (shard // 2) % 2, shard % 2

    def at(r, yy, hh, cc):
        return (r, (((yy + N_Y) % N_Y) * 2 + hh) * 2 + cc)

    bit = (rep // 2**level) % 2
    pair_rep = rep + (1 - 2 * bit) * 2**level
    up, down = at(rep, y + 1, half, core), at(rep, y - 1, half, core)
    across = at(rep, y, 1 - half, core)
    other = at(rep, y, half, 1 - core)
    pair = at(pair_rep, y, half, core)
    friends, far_friends = [up, down, other, pair], [across]
    if along_x:
        pair_up, pair_down = at(pair_rep, y + 1, half, core), at(pair_rep, y - 1, half, core)
        friends = friends + [pair_up, pair_down]
    else:
        pair_across = at(pair_rep, y, 1 - half, core)
        far_friends = far_friends + [pair_across]

    def signal(semaphore, devices):
        for device in devices:
            pl.semaphore_signal(semaphore, 1, device_id=device, device_id_type=MESH)

    plane, pair_plane = rep // N_X, pair_rep // N_X
    early = [plane < ahead_of]
    if not along_x:
        early = early + [jnp.where(half == 0, plane, pair_plane) < ahead_of]
    knows = jnp.logical_or(half == 1, plane >= ahead_of)
    barrier = pltpu.get_barrier_semaphore()
    for device, ahead in zip(far_friends, early):
        pl.when(jnp.logical_or(half == 0, jnp.logical_not(ahead)))(
            partial(signal, barrier, [device])
        )
    signal(barrier, friends)

    def fetch(src, dst, i):
        copy = pltpu.make_async_copy(src, dst, local_sem.at[i])
        copy.start()
        return copy

    load_hid = fetch(hid_ref, hid, 0)
    load_d = fetch(d_ref, d.at[0], 1)

    leaving, landing = {}, {}

    def send(src, dst, device, leave, land, start=True):
        copy = pltpu.make_async_remote_copy(
            src,
            dst,
            send_sem.at[leaving.setdefault(leave, len(leaving))],
            recv_sem.at[landing.setdefault(land, len(landing))],
            device_id=device,
            device_id_type=MESH,
        )
        if start:
            copy.start()
        return copy

    def landed(land, whole):
        pltpu.make_async_copy(whole, whole, recv_sem.at[landing[land]]).wait()

    pl.semaphore_wait(barrier, len(friends) + knows.astype(jnp.int32) * len(far_friends))
    for device, ahead in zip(far_friends, early):
        pl.when(jnp.logical_and(half == 1, ahead))(partial(signal, ready, [device]))

    def piece(q):
        n = blk // W_CHUNKS
        return pl.ds(q * n, n)

    w_cross = [
        send(w_ref.at[piece(q)], wts.at[4, piece(q)], across, "w", f"w{q}", start=False)
        for q in range(W_CHUNKS)
    ]

    def start_w():
        for copy in w_cross:
            copy.start()

    pl.when(knows)(start_w)
    lower, upper = pl.ds(0, mid), pl.ds(mid, mid)

    for i, (s_up, s_down) in enumerate(((lower, upper), (upper, lower))):
        send(w_ref.at[s_up], wts.at[3, s_up], up, "near", f"near{i}")
        send(w_ref.at[s_down], wts.at[1, s_down], down, "near", f"near{i}")

    load_w = fetch(w_ref, wts.at[0], 2)
    load_mom = fetch(mom_ref, mom, 3)
    load_d.wait()
    core_d = send(d.at[0], d.at[1], other, "d", "d")

    step = 32

    def norm_rows(i, carry):
        here = pl.ds(pl.multiple_of(i * step, step), step)
        total = jnp.zeros((step, blk), F32)
        for j in range(feats // blk):
            v = hid[here, j * blk : (j + 1) * blk].astype(F32)
            total = total + v * v
        scale = lax.rsqrt(jnp.sum(total, axis=1, keepdims=True) * (1.0 / feats) + 1e-05)
        for j in range(2 * N_Y):
            for mine in range(2):
                which = core if mine else 1 - core
                span = pl.ds(pl.multiple_of((2 * j + which) * blk, blk), blk)
                out = (hid[here, span].astype(F32) * scale * gain_ref[:, span]).astype(BF16)
                if mine:
                    normed[0, j % 2, j // 2, here] = out
                else:
                    to_core[j % 2, j // 2, here] = out
        return carry

    load_hid.wait()
    lax.fori_loop(0, rows // step, norm_rows, 0)
    core_n = {
        1: send(to_core.at[1 - half], normed.at[1, 1 - half], other, "n", "n1"),
        0: send(to_core.at[half], normed.at[1, half], other, "n", "n0"),
    }

    def tokens_of(t, k, far):
        return normed[t, 1 - half if far else half, (y + k) % N_Y]

    def grad_block(k, far):
        return sum(
            lax.dot_general(
                tokens_of(t, k, far), d[t], (((0,), (0,)), ((), ())), preferred_element_type=F32
            )
            for t in range(2)
        )

    mine = pl.ds(pl.multiple_of(bit * mid, mid), mid)
    theirs = pl.ds(pl.multiple_of((1 - bit) * mid, mid), mid)
    first, own = {}, {}

    def send_side(far, way, part_of):
        src = side_out.at[far, way, part_of]
        if along_x:
            ends = ((up, down)[way], (pair_up, pair_down)[way])
            for i, span in enumerate((mine, theirs)):
                dst = side_in.at[far, way, part_of, pl.ds(i * mid, mid)]
                send(src.at[span], dst, ends[i], "side", f"side{far}")
        else:
            send(src, side_in.at[far, way, part_of], (up, down)[way], "side", f"side{far}")

    def reduce_first(far):
        block = grad_block(2, far).astype(BF16)
        first_out[far, 0] = block[:, :cols]
        first_out[far, 1] = block[:, cols:]
        first[far] = [
            send(first_out.at[far, 0], first_in.at[far, 0], up, "first", f"first{far}0"),
            send(first_out.at[far, 1], first_in.at[far, 1], down, "first", f"first{far}1"),
        ]
        for way, k in ((0, 1), (1, 3)):
            block = grad_block(k, far)
            parts = (block[:, :cols], block[:, cols:])
            side_out[far, way, 1 - way] = parts[1 - way].astype(BF16)
            send_side(far, way, 1 - way)
            keep_side[far, way] = parts[way]
        block = grad_block(0, far)
        if not far:
            block = block + 0.9 * mom[...]
        keep[far] = block
        if along_x:
            own_out[far] = keep[far, theirs].astype(BF16)
            own[far] = send(own_out.at[far], own_in.at[far], pair, "own", f"own{far}")

    def reduce_second(far):
        for way in range(2):
            first[far][way].wait_recv()
            side_out[far, way, way] = (
                keep_side[far, way] + first_in[far, way].astype(F32)
            ).astype(BF16)
            send_side(far, way, way)

    def reduced(far, span, copies):
        total = keep[far, span]
        for at_row in copies:
            for way in range(2):
                total = total + jnp.concatenate(
                    [side_in[far, way, c, pl.ds(at_row, mid)] for c in range(2)], axis=1
                ).astype(F32)
        return total

    def wait_reduced(far):
        landed(f"side{far}", side_in.at[far])
        if along_x:
            own[far].wait_recv()

    def project(k, far, begin=False, tokens=(0, 1)):
        for t in tokens:
            new = jnp.dot(tokens_of(t, k, far), wts[4 * far + k], preferred_element_type=F32)
            part[t] = new if begin else part[t] + new

    def back_rows(i):
        n = mid // BACK
        return pl.ds(i * n, n)

    core_d.wait_recv()
    core_n[1].wait_recv()
    reduce_first(1)
    core_n[0].wait_recv()
    load_w.wait()
    load_mom.wait()
    project(0, 0, True)
    reduce_second(1)
    reduce_first(0)


    def start_lower():
        pl.semaphore_wait(ready, len(far_friends))
        start_w()

    pl.when(jnp.logical_not(knows))(start_lower)
    wait_reduced(1)
    if along_x:
        z_out[0] = (reduced(1, mine, (0, mid)) + own_in[1].astype(F32)).astype(BF16)
        for i in range(BACK):
            send(z_out.at[0, back_rows(i)], z_in.at[0, back_rows(i)], across, "z", f"z{i}")
    else:
        for i, span in enumerate((mine, theirs)):
            start = bit * mid if i == 0 else (1 - bit) * mid
            z_out[i] = reduced(1, span, (pl.multiple_of(start, mid),)).astype(BF16)
        for q in range(BACK):
            for i, device in enumerate((across, pair_across)):
                send(z_out.at[i, back_rows(q)], z_in.at[i, back_rows(q)], device, "z", f"z{q}")

    far_up, far_down = {}, {}

    def spread(q):
        w_cross[q].wait_recv()
        s = piece(q)
        for way in (q % 2, 1 - q % 2):
            if way == 0:
                land = f"far{q}" if q % 2 == 0 else "far"
                far_up[q] = send(wts.at[4, s], wts.at[7, s], up, "far", land)
            else:
                land = f"far{q}" if q % 2 else "far"
                far_down[q] = send(wts.at[4, s], wts.at[5, s], down, "far", land)

    def relay(q):
        s = piece(q)
        if q % 2 == 0:
            far_up[q].wait_recv()
            send(wts.at[7, s], wts.at[6, s], up, "far_relay", "far_relay")
        else:
            far_down[q].wait_recv()
            send(wts.at[5, s], wts.at[6, s], down, "far_relay", "far_relay")

    spread(0)
    reduce_second(0)
    spread(1)
    relay(0)
    wait_reduced(0)
    if along_x:
        keep[0, mine] = reduced(0, mine, (0, mid)) + own_in[0].astype(F32)
    else:
        z_out[2] = reduced(0, theirs, (pl.multiple_of((1 - bit) * mid, mid),)).astype(BF16)
        for q in range(BACK):
            send(z_out.at[2, back_rows(q)], z_in.at[2, back_rows(q)], pair, "z", f"z{q}")
        keep[0, mine] = reduced(0, mine, (pl.multiple_of(bit * mid, mid),))
    landed("near0", wts.at[1])
    send(wts.at[3, lower], wts.at[2, lower], up, "near_relay", "near_relay")
    send(wts.at[1, upper], wts.at[2, upper], down, "near_relay", "near_relay")
    spread(2)
    relay(1)
    landed("near1", wts.at[1])
    project(1, 0)
    project(3, 0)
    spread(3)
    relay(2)
    project(0, 1)
    relay(3)
    landed("near_relay", wts.at[2])
    project(2, 0)
    landed("far", wts.at[5])
    project(1, 1)
    project(3, 1)

    def finish(q):
        s = back_rows(q)
        n = mid // BACK
        total = keep[0, pl.ds(pl.multiple_of(bit * mid + q * n, n), n)]
        if along_x:
            landed(f"z{q}", z_in.at[0, s])
            total = total + z_in[0, s].astype(F32)
        else:
            landed(f"z{q}", z_in.at[:, s])
            total = total + z_in[0, s].astype(F32) + z_in[1, s].astype(F32) + z_in[2, s].astype(F32)
        result = 0.5 * total
        back_out[s] = result.astype(BF16)
        send(back_out.at[s], back_in.at[s], pair, "back", "back")
        averaged_ref[pl.ds(pl.multiple_of(bit * mid + q * n, n), n)] = result

    for q in range(BACK):
        finish(q)
    landed("far_relay", wts.at[6])
    project(2, 1, tokens=(1,))
    vals_send = send(part.at[1], vals_in, other, "vals", "vals")
    project(2, 1, tokens=(0,))
    vals_send.wait_recv()
    values_ref[...] = (part[0] + vals_in[...]).astype(BF16)
    landed("back", back_in)
    averaged_ref[theirs] = back_in[...].astype(F32)

    total_of = {
        "w": wts.at[4],
        "d": d.at[0],
        "n": to_core,
        "first": first_out,
        "side": side_out,
        "own": own_out,
        "z": z_out.at[0] if along_x else z_out,
        "far": wts.at[pl.ds(4, 2)],
        "far_relay": wts.at[6],
        "near": wts.at[pl.ds(0, 2)],
        "near_relay": wts.at[2],
        "vals": vals_in,
        "back": back_in,
    }
    assert len(leaving) <= N_SEND and len(landing) <= N_RECV
    for leave, i in leaving.items():
        pltpu.make_async_copy(total_of[leave], total_of[leave], send_sem.at[i]).wait()


def fused(level, hidden, gain, weight, cotangent, momentum):
    rows, feats = hidden.shape
    blk, kv = weight.shape
    mid, cols = blk // 2, kv // 2
    anywhere = pl.BlockSpec(memory_space=pl.ANY)
    vmem = pl.BlockSpec(memory_space=pltpu.VMEM)
    return pl.pallas_call(
        partial(kernel, level),
        name=f"layer_level_{level}",
        out_shape=(
            jax.ShapeDtypeStruct((rows, kv), BF16),
            jax.ShapeDtypeStruct((blk, kv), F32),
        ),
        in_specs=[anywhere, vmem, anywhere, anywhere, anywhere],
        out_specs=(vmem, vmem),
        scratch_shapes=[
            pltpu.VMEM((rows, feats), BF16),
            pltpu.VMEM((blk, kv), F32),
            pltpu.VMEM((2, 2, N_Y, rows, blk), BF16),
            pltpu.VMEM((2, N_Y, rows, blk), BF16),
            pltpu.VMEM((2, rows, kv), BF16),
            pltpu.VMEM((2 * N_Y, blk, kv), BF16),
            pltpu.VMEM((2, rows, kv), F32),
            pltpu.VMEM((rows, kv), F32),
            pltpu.VMEM((2, blk, kv), F32),
            pltpu.VMEM((2, 2, blk, cols), F32),
            pltpu.VMEM((2, 2, blk, cols), BF16),
            pltpu.VMEM((2, 2, blk, cols), BF16),
            pltpu.VMEM((2, 2, 2, blk, cols), BF16),
            pltpu.VMEM((2, 2, 2, blk, cols), BF16),
            pltpu.VMEM((2, mid, kv), BF16),
            pltpu.VMEM((2, mid, kv), BF16),
            pltpu.VMEM((3, mid, kv), BF16),
            pltpu.VMEM((3, mid, kv), BF16),
            pltpu.VMEM((mid, kv), BF16),
            pltpu.VMEM((mid, kv), BF16),
            pltpu.SemaphoreType.DMA((4,)),
            pltpu.SemaphoreType.DMA((N_SEND,)),
            pltpu.SemaphoreType.DMA((N_RECV,)),
            pltpu.SemaphoreType.REGULAR,
        ],
        compiler_params=pltpu.CompilerParams(
            collective_id=level, has_side_effects=True, vmem_limit_bytes=40 << 20
        ),
    )(hidden, gain, weight, cotangent, momentum)


def store_kernel(values_ref, averaged_ref, values_out, averaged_out, sems):
    copies = [
        pltpu.make_async_copy(values_ref, values_out, sems.at[0]),
        pltpu.make_async_copy(averaged_ref, averaged_out, sems.at[1]),
    ]
    for copy in copies:
        copy.start()
    for copy in copies:
        copy.wait()


def store(values, averaged):
    anywhere = pl.BlockSpec(memory_space=pl.ANY)
    return pl.pallas_call(
        store_kernel,
        name="store",
        out_shape=(
            jax.ShapeDtypeStruct(values.shape, values.dtype),
            jax.ShapeDtypeStruct(averaged.shape, averaged.dtype),
        ),
        in_specs=[anywhere, anywhere],
        out_specs=(anywhere, anywhere),
        scratch_shapes=[pltpu.SemaphoreType.DMA((2,))],
    )(values, averaged)


def local(hidden_in, norm_gain, w_value, d_values, momentum, step):
    levels = lax.axis_size("rep").bit_length() - 1
    branches = [partial(fused, level) for level in range(levels)]
    values, averaged = lax.switch(
        lax.rem(step, levels), branches, hidden_in[0], norm_gain, w_value[0], d_values[0], momentum[0]
    )
    values, averaged = store(values, averaged)
    return (values[None], averaged[None])


def solution(mesh):
    placed = (
        P("rep", "fsdp", None),
        P("rep", None),
        P("rep", "fsdp", None),
        P("rep", "fsdp", None),
        P("rep", "fsdp", None),
        P(),
    )
    return jax.shard_map(
        local,
        mesh=mesh,
        in_specs=placed,
        out_specs=(P("rep", "fsdp", None), P("rep", "fsdp", None)),
        check_vma=False,
    )
```

```python
from functools import partial

import jax
import jax.numpy as jnp
from jax import lax
from jax.experimental import pallas as pl
from jax.experimental.pallas import tpu as pltpu
from jax.sharding import PartitionSpec as P

MESH = pl.DeviceIdType.MESH
F32 = jnp.float32
BF16 = jnp.bfloat16
N_X = 4
N_Y = 4
X_LEVELS = 2
W_CHUNKS = 4
BACK = 2
EARLY = 4
N_SEND, N_RECV = 13, 32


def kernel(
    level, hid_ref, gain_ref, w_ref, d_ref, mom_ref, values_ref, averaged_ref,
    hid, mom, normed, to_core, d, wts, part, vals_in,
    keep, keep_side, first_out, first_in, side_out, side_in, own_out, own_in,
    z_out, z_in, back_out, back_in,
    local_sem, send_sem, recv_sem, ready,
):
    along_x = level < X_LEVELS
    ahead_of = EARLY if along_x or 2**level < EARLY * N_X else 0
    rows, feats = hid.shape
    blk, kv = w_ref.shape
    mid, cols = blk // 2, kv // 2
    rep, shard = lax.axis_index("rep"), lax.axis_index("fsdp")
    y, half, core = shard // 4, (shard // 2) % 2, shard % 2

    def at(r, yy, hh, cc):
        return (r, (((yy + N_Y) % N_Y) * 2 + hh) * 2 + cc)

    bit = (rep // 2**level) % 2
    pair_rep = rep + (1 - 2 * bit) * 2**level
    up, down = at(rep, y + 1, half, core), at(rep, y - 1, half, core)
    across = at(rep, y, 1 - half, core)
    other = at(rep, y, half, 1 - core)
    pair = at(pair_rep, y, half, core)
    friends, far_friends = [up, down, other, pair], [across]
    if along_x:
        pair_up, pair_down = at(pair_rep, y + 1, half, core), at(pair_rep, y - 1, half, core)
        friends = friends + [pair_up, pair_down]
    else:
        pair_across = at(pair_rep, y, 1 - half, core)
        far_friends = far_friends + [pair_across]

    def signal(semaphore, devices):
        for device in devices:
            pl.semaphore_signal(semaphore, 1, device_id=device, device_id_type=MESH)

    plane, pair_plane = rep // N_X, pair_rep // N_X
    early = [plane < ahead_of]
    if not along_x:
        early = early + [jnp.where(half == 0, plane, pair_plane) < ahead_of]
    knows = jnp.logical_or(half == 1, plane >= ahead_of)
    barrier = pltpu.get_barrier_semaphore()
    for device, ahead in zip(far_friends, early):
        pl.when(jnp.logical_or(half == 0, jnp.logical_not(ahead)))(
            partial(signal, barrier, [device])
        )
    signal(barrier, friends)

    def fetch(src, dst, i):
        copy = pltpu.make_async_copy(src, dst, local_sem.at[i])
        copy.start()
        return copy

    load_hid = fetch(hid_ref, hid, 0)
    load_d = fetch(d_ref, d.at[0], 1)

    leaving, landing = {}, {}

    def send(src, dst, device, leave, land, start=True):
        copy = pltpu.make_async_remote_copy(
            src,
            dst,
            send_sem.at[leaving.setdefault(leave, len(leaving))],
            recv_sem.at[landing.setdefault(land, len(landing))],
            device_id=device,
            device_id_type=MESH,
        )
        if start:
            copy.start()
        return copy

    def landed(land, whole):
        pltpu.make_async_copy(whole, whole, recv_sem.at[landing[land]]).wait()

    pl.semaphore_wait(barrier, len(friends) + knows.astype(jnp.int32) * len(far_friends))
    for device, ahead in zip(far_friends, early):
        pl.when(jnp.logical_and(half == 1, ahead))(partial(signal, ready, [device]))

    def piece(q):
        n = blk // W_CHUNKS
        return pl.ds(q * n, n)

    w_cross = [
        send(w_ref.at[piece(q)], wts.at[4, piece(q)], across, "w", f"w{q}", start=False)
        for q in range(W_CHUNKS)
    ]

    def start_w():
        for copy in w_cross:
            copy.start()

    pl.when(knows)(start_w)
    lower, upper = pl.ds(0, mid), pl.ds(mid, mid)

    def send_near():
        for i, (s_up, s_down) in enumerate(((lower, upper), (upper, lower))):
            send(w_ref.at[s_up], wts.at[3, s_up], up, "near", f"near{i}")
            send(w_ref.at[s_down], wts.at[1, s_down], down, "near", f"near{i}")

    if along_x:
        send_near()

    load_w = fetch(w_ref, wts.at[0], 2)
    load_mom = fetch(mom_ref, mom, 3)
    load_d.wait()
    core_d = send(d.at[0], d.at[1], other, "d", "d")

    step = 32

    def norm_rows(i, carry):
        here = pl.ds(pl.multiple_of(i * step, step), step)
        total = jnp.zeros((step, blk), F32)
        for j in range(feats // blk):
            v = hid[here, j * blk : (j + 1) * blk].astype(F32)
            total = total + v * v
        scale = lax.rsqrt(jnp.sum(total, axis=1, keepdims=True) * (1.0 / feats) + 1e-05)
        for j in range(2 * N_Y):
            for mine in range(2):
                which = core if mine else 1 - core
                span = pl.ds(pl.multiple_of((2 * j + which) * blk, blk), blk)
                out = (hid[here, span].astype(F32) * scale * gain_ref[:, span]).astype(BF16)
                if mine:
                    normed[0, j % 2, j // 2, here] = out
                else:
                    to_core[j % 2, j // 2, here] = out
        return carry

    load_hid.wait()
    lax.fori_loop(0, rows // step, norm_rows, 0)
    core_n = {
        1: send(to_core.at[1 - half], normed.at[1, 1 - half], other, "n", "n1"),
        0: send(to_core.at[half], normed.at[1, half], other, "n", "n0"),
    }

    def tokens_of(t, k, far):
        return normed[t, 1 - half if far else half, (y + k) % N_Y]

    def grad_block(k, far):
        return sum(
            lax.dot_general(
                tokens_of(t, k, far), d[t], (((0,), (0,)), ((), ())), preferred_element_type=F32
            )
            for t in range(2)
        )

    mine = pl.ds(pl.multiple_of(bit * mid, mid), mid)
    theirs = pl.ds(pl.multiple_of((1 - bit) * mid, mid), mid)
    first, own = {}, {}

    def send_side(far, way, part_of):
        src = side_out.at[far, way, part_of]
        if along_x:
            ends = ((up, down)[way], (pair_up, pair_down)[way])
            for i, span in enumerate((mine, theirs)):
                dst = side_in.at[far, way, part_of, pl.ds(i * mid, mid)]
                send(src.at[span], dst, ends[i], "side", f"side{far}")
        else:
            send(src, side_in.at[far, way, part_of], (up, down)[way], "side", f"side{far}")

    def reduce_first(far):
        block = grad_block(2, far).astype(BF16)
        first_out[far, 0] = block[:, :cols]
        first_out[far, 1] = block[:, cols:]
        first[far] = [
            send(first_out.at[far, 0], first_in.at[far, 0], up, "first", f"first{far}0"),
            send(first_out.at[far, 1], first_in.at[far, 1], down, "first", f"first{far}1"),
        ]
        for way, k in ((0, 1), (1, 3)):
            block = grad_block(k, far)
            parts = (block[:, :cols], block[:, cols:])
            side_out[far, way, 1 - way] = parts[1 - way].astype(BF16)
            send_side(far, way, 1 - way)
            keep_side[far, way] = parts[way]
        block = grad_block(0, far)
        if not far:
            block = block + 0.9 * mom[...]
        keep[far] = block
        if along_x:
            own_out[far] = keep[far, theirs].astype(BF16)
            own[far] = send(own_out.at[far], own_in.at[far], pair, "own", f"own{far}")

    def reduce_second(far):
        for way in range(2):
            first[far][way].wait_recv()
            side_out[far, way, way] = (
                keep_side[far, way] + first_in[far, way].astype(F32)
            ).astype(BF16)
            send_side(far, way, way)

    def reduced(far, span, copies):
        total = keep[far, span]
        for at_row in copies:
            for way in range(2):
                total = total + jnp.concatenate(
                    [side_in[far, way, c, pl.ds(at_row, mid)] for c in range(2)], axis=1
                ).astype(F32)
        return total

    def wait_reduced(far):
        landed(f"side{far}", side_in.at[far])
        if along_x:
            own[far].wait_recv()

    def project(k, far, begin=False, tokens=(0, 1)):
        for t in tokens:
            new = jnp.dot(tokens_of(t, k, far), wts[4 * far + k], preferred_element_type=F32)
            part[t] = new if begin else part[t] + new

    def back_rows(i):
        n = mid // BACK
        return pl.ds(i * n, n)

    core_d.wait_recv()
    core_n[1].wait_recv()
    reduce_first(1)
    core_n[0].wait_recv()
    load_w.wait()
    load_mom.wait()
    project(0, 0, True)
    reduce_second(1)
    reduce_first(0)


    def start_lower():
        pl.semaphore_wait(ready, len(far_friends))
        start_w()

    pl.when(jnp.logical_not(knows))(start_lower)
    wait_reduced(1)
    if along_x:
        z_out[0] = (reduced(1, mine, (0, mid)) + own_in[1].astype(F32)).astype(BF16)
        for i in range(BACK):
            send(z_out.at[0, back_rows(i)], z_in.at[0, back_rows(i)], across, "z", f"z{i}")
    else:
        for i, span in enumerate((mine, theirs)):
            start = bit * mid if i == 0 else (1 - bit) * mid
            z_out[i] = reduced(1, span, (pl.multiple_of(start, mid),)).astype(BF16)
        for q in range(BACK):
            for i, device in enumerate((across, pair_across)):
                send(z_out.at[i, back_rows(q)], z_in.at[i, back_rows(q)], device, "z", f"z{q}")

    far_up, far_down = {}, {}

    def spread(q):
        w_cross[q].wait_recv()
        s = piece(q)
        for way in (q % 2, 1 - q % 2):
            if way == 0:
                land = f"far{q}" if q % 2 == 0 else "far"
                far_up[q] = send(wts.at[4, s], wts.at[7, s], up, "far", land)
            else:
                land = f"far{q}" if q % 2 else "far"
                far_down[q] = send(wts.at[4, s], wts.at[5, s], down, "far", land)

    def relay(q):
        s = piece(q)
        if q % 2 == 0:
            far_up[q].wait_recv()
            send(wts.at[7, s], wts.at[6, s], up, "far_relay", "far_relay")
        else:
            far_down[q].wait_recv()
            send(wts.at[5, s], wts.at[6, s], down, "far_relay", "far_relay")

    spread(0)
    reduce_second(0)
    if not along_x:
        send_near()
    spread(1)
    relay(0)
    wait_reduced(0)
    if along_x:
        keep[0, mine] = reduced(0, mine, (0, mid)) + own_in[0].astype(F32)
    else:
        z_out[2] = reduced(0, theirs, (pl.multiple_of((1 - bit) * mid, mid),)).astype(BF16)
        for q in range(BACK):
            send(z_out.at[2, back_rows(q)], z_in.at[2, back_rows(q)], pair, "z", f"z{q}")
        keep[0, mine] = reduced(0, mine, (pl.multiple_of(bit * mid, mid),))
    landed("near0", wts.at[1])
    send(wts.at[3, lower], wts.at[2, lower], up, "near_relay", "near_relay")
    send(wts.at[1, upper], wts.at[2, upper], down, "near_relay", "near_relay")
    spread(2)
    relay(1)
    landed("near1", wts.at[1])
    project(1, 0)
    project(3, 0)
    spread(3)
    relay(2)
    project(0, 1)
    relay(3)
    landed("near_relay", wts.at[2])
    project(2, 0)
    landed("far", wts.at[5])
    project(1, 1)
    project(3, 1)

    def finish(q):
        s = back_rows(q)
        n = mid // BACK
        total = keep[0, pl.ds(pl.multiple_of(bit * mid + q * n, n), n)]
        if along_x:
            landed(f"z{q}", z_in.at[0, s])
            total = total + z_in[0, s].astype(F32)
        else:
            landed(f"z{q}", z_in.at[:, s])
            total = total + z_in[0, s].astype(F32) + z_in[1, s].astype(F32) + z_in[2, s].astype(F32)
        result = 0.5 * total
        back_out[s] = result.astype(BF16)
        send(back_out.at[s], back_in.at[s], pair, "back", "back")
        averaged_ref[pl.ds(pl.multiple_of(bit * mid + q * n, n), n)] = result

    for q in range(BACK):
        finish(q)
    landed("far_relay", wts.at[6])
    project(2, 1, tokens=(1,))
    vals_send = send(part.at[1], vals_in, other, "vals", "vals")
    project(2, 1, tokens=(0,))
    vals_send.wait_recv()
    values_ref[...] = (part[0] + vals_in[...]).astype(BF16)
    landed("back", back_in)
    averaged_ref[theirs] = back_in[...].astype(F32)

    total_of = {
        "w": wts.at[4],
        "d": d.at[0],
        "n": to_core,
        "first": first_out,
        "side": side_out,
        "own": own_out,
        "z": z_out.at[0] if along_x else z_out,
        "far": wts.at[pl.ds(4, 2)],
        "far_relay": wts.at[6],
        "near": wts.at[pl.ds(0, 2)],
        "near_relay": wts.at[2],
        "vals": vals_in,
        "back": back_in,
    }
    assert len(leaving) <= N_SEND and len(landing) <= N_RECV
    for leave, i in leaving.items():
        pltpu.make_async_copy(total_of[leave], total_of[leave], send_sem.at[i]).wait()


def fused(level, hidden, gain, weight, cotangent, momentum):
    rows, feats = hidden.shape
    blk, kv = weight.shape
    mid, cols = blk // 2, kv // 2
    anywhere = pl.BlockSpec(memory_space=pl.ANY)
    vmem = pl.BlockSpec(memory_space=pltpu.VMEM)
    return pl.pallas_call(
        partial(kernel, level),
        name=f"layer_level_{level}",
        out_shape=(
            jax.ShapeDtypeStruct((rows, kv), BF16),
            jax.ShapeDtypeStruct((blk, kv), F32),
        ),
        in_specs=[anywhere, vmem, anywhere, anywhere, anywhere],
        out_specs=(vmem, vmem),
        scratch_shapes=[
            pltpu.VMEM((rows, feats), BF16),
            pltpu.VMEM((blk, kv), F32),
            pltpu.VMEM((2, 2, N_Y, rows, blk), BF16),
            pltpu.VMEM((2, N_Y, rows, blk), BF16),
            pltpu.VMEM((2, rows, kv), BF16),
            pltpu.VMEM((2 * N_Y, blk, kv), BF16),
            pltpu.VMEM((2, rows, kv), F32),
            pltpu.VMEM((rows, kv), F32),
            pltpu.VMEM((2, blk, kv), F32),
            pltpu.VMEM((2, 2, blk, cols), F32),
            pltpu.VMEM((2, 2, blk, cols), BF16),
            pltpu.VMEM((2, 2, blk, cols), BF16),
            pltpu.VMEM((2, 2, 2, blk, cols), BF16),
            pltpu.VMEM((2, 2, 2, blk, cols), BF16),
            pltpu.VMEM((2, mid, kv), BF16),
            pltpu.VMEM((2, mid, kv), BF16),
            pltpu.VMEM((3, mid, kv), BF16),
            pltpu.VMEM((3, mid, kv), BF16),
            pltpu.VMEM((mid, kv), BF16),
            pltpu.VMEM((mid, kv), BF16),
            pltpu.SemaphoreType.DMA((4,)),
            pltpu.SemaphoreType.DMA((N_SEND,)),
            pltpu.SemaphoreType.DMA((N_RECV,)),
            pltpu.SemaphoreType.REGULAR,
        ],
        compiler_params=pltpu.CompilerParams(
            collective_id=level, has_side_effects=True, vmem_limit_bytes=40 << 20
        ),
    )(hidden, gain, weight, cotangent, momentum)


def store_kernel(values_ref, averaged_ref, values_out, averaged_out, sems):
    copies = [
        pltpu.make_async_copy(values_ref, values_out, sems.at[0]),
        pltpu.make_async_copy(averaged_ref, averaged_out, sems.at[1]),
    ]
    for copy in copies:
        copy.start()
    for copy in copies:
        copy.wait()


def store(values, averaged):
    anywhere = pl.BlockSpec(memory_space=pl.ANY)
    return pl.pallas_call(
        store_kernel,
        name="store",
        out_shape=(
            jax.ShapeDtypeStruct(values.shape, values.dtype),
            jax.ShapeDtypeStruct(averaged.shape, averaged.dtype),
        ),
        in_specs=[anywhere, anywhere],
        out_specs=(anywhere, anywhere),
        scratch_shapes=[pltpu.SemaphoreType.DMA((2,))],
    )(values, averaged)


def local(hidden_in, norm_gain, w_value, d_values, momentum, step):
    levels = lax.axis_size("rep").bit_length() - 1
    branches = [partial(fused, level) for level in range(levels)]
    values, averaged = lax.switch(
        lax.rem(step, levels), branches, hidden_in[0], norm_gain, w_value[0], d_values[0], momentum[0]
    )
    values, averaged = store(values, averaged)
    return (values[None], averaged[None])


def solution(mesh):
    placed = (
        P("rep", "fsdp", None),
        P("rep", None),
        P("rep", "fsdp", None),
        P("rep", "fsdp", None),
        P("rep", "fsdp", None),
        P(),
    )
    return jax.shard_map(
        local,
        mesh=mesh,
        in_specs=placed,
        out_specs=(P("rep", "fsdp", None), P("rep", "fsdp", None)),
        check_vma=False,
    )
```

```python
from functools import partial

import jax
import jax.numpy as jnp
from jax import lax
from jax.experimental import pallas as pl
from jax.experimental.pallas import tpu as pltpu
from jax.sharding import PartitionSpec as P

MESH = pl.DeviceIdType.MESH
F32 = jnp.float32
BF16 = jnp.bfloat16
N_X = 4
N_Y = 4
X_LEVELS = 2
W_CHUNKS = 4
BACK = 4
EARLY = 4
N_SEND, N_RECV = 13, 32


def kernel(
    level, hid_ref, gain_ref, w_ref, d_ref, mom_ref, values_ref, averaged_ref,
    hid, mom, normed, to_core, d, wts, part, vals_in,
    keep, keep_side, first_out, first_in, side_out, side_in, own_out, own_in,
    z_out, z_in, back_out, back_in,
    local_sem, send_sem, recv_sem, ready,
):
    along_x = level < X_LEVELS
    ahead_of = EARLY if along_x or 2**level < EARLY * N_X else 0
    rows, feats = hid.shape
    blk, kv = w_ref.shape
    mid, cols = blk // 2, kv // 2
    rep, shard = lax.axis_index("rep"), lax.axis_index("fsdp")
    y, half, core = shard // 4, (shard // 2) % 2, shard % 2

    def at(r, yy, hh, cc):
        return (r, (((yy + N_Y) % N_Y) * 2 + hh) * 2 + cc)

    bit = (rep // 2**level) % 2
    pair_rep = rep + (1 - 2 * bit) * 2**level
    up, down = at(rep, y + 1, half, core), at(rep, y - 1, half, core)
    across = at(rep, y, 1 - half, core)
    other = at(rep, y, half, 1 - core)
    pair = at(pair_rep, y, half, core)
    friends, far_friends = [up, down, other, pair], [across]
    if along_x:
        pair_up, pair_down = at(pair_rep, y + 1, half, core), at(pair_rep, y - 1, half, core)
        friends = friends + [pair_up, pair_down]
    else:
        pair_across = at(pair_rep, y, 1 - half, core)
        far_friends = far_friends + [pair_across]

    def signal(semaphore, devices):
        for device in devices:
            pl.semaphore_signal(semaphore, 1, device_id=device, device_id_type=MESH)

    plane, pair_plane = rep // N_X, pair_rep // N_X
    early = [plane < ahead_of]
    if not along_x:
        early = early + [jnp.where(half == 0, plane, pair_plane) < ahead_of]
    knows = jnp.logical_or(half == 1, plane >= ahead_of)
    barrier = pltpu.get_barrier_semaphore()
    for device, ahead in zip(far_friends, early):
        pl.when(jnp.logical_or(half == 0, jnp.logical_not(ahead)))(
            partial(signal, barrier, [device])
        )
    signal(barrier, friends)

    def fetch(src, dst, i):
        copy = pltpu.make_async_copy(src, dst, local_sem.at[i])
        copy.start()
        return copy

    load_hid = fetch(hid_ref, hid, 0)
    load_d = fetch(d_ref, d.at[0], 1)

    leaving, landing = {}, {}

    def send(src, dst, device, leave, land, start=True):
        copy = pltpu.make_async_remote_copy(
            src,
            dst,
            send_sem.at[leaving.setdefault(leave, len(leaving))],
            recv_sem.at[landing.setdefault(land, len(landing))],
            device_id=device,
            device_id_type=MESH,
        )
        if start:
            copy.start()
        return copy

    def landed(land, whole):
        pltpu.make_async_copy(whole, whole, recv_sem.at[landing[land]]).wait()

    pl.semaphore_wait(barrier, len(friends) + knows.astype(jnp.int32) * len(far_friends))
    for device, ahead in zip(far_friends, early):
        pl.when(jnp.logical_and(half == 1, ahead))(partial(signal, ready, [device]))

    def piece(q):
        n = blk // W_CHUNKS
        return pl.ds(q * n, n)

    w_cross = [
        send(w_ref.at[piece(q)], wts.at[4, piece(q)], across, "w", f"w{q}", start=False)
        for q in range(W_CHUNKS)
    ]

    def start_w():
        for copy in w_cross:
            copy.start()

    pl.when(knows)(start_w)
    lower, upper = pl.ds(0, mid), pl.ds(mid, mid)

    def send_near():
        for i, (s_up, s_down) in enumerate(((lower, upper), (upper, lower))):
            send(w_ref.at[s_up], wts.at[3, s_up], up, "near", f"near{i}")
            send(w_ref.at[s_down], wts.at[1, s_down], down, "near", f"near{i}")

    if along_x:
        send_near()

    load_w = fetch(w_ref, wts.at[0], 2)
    load_mom = fetch(mom_ref, mom, 3)
    load_d.wait()
    core_d = send(d.at[0], d.at[1], other, "d", "d")

    step = 32

    def norm_rows(i, carry):
        here = pl.ds(pl.multiple_of(i * step, step), step)
        total = jnp.zeros((step, blk), F32)
        for j in range(feats // blk):
            v = hid[here, j * blk : (j + 1) * blk].astype(F32)
            total = total + v * v
        scale = lax.rsqrt(jnp.sum(total, axis=1, keepdims=True) * (1.0 / feats) + 1e-05)
        for j in range(2 * N_Y):
            for mine in range(2):
                which = core if mine else 1 - core
                span = pl.ds(pl.multiple_of((2 * j + which) * blk, blk), blk)
                out = (hid[here, span].astype(F32) * scale * gain_ref[:, span]).astype(BF16)
                if mine:
                    normed[0, j % 2, j // 2, here] = out
                else:
                    to_core[j % 2, j // 2, here] = out
        return carry

    load_hid.wait()
    lax.fori_loop(0, rows // step, norm_rows, 0)
    core_n = {
        1: send(to_core.at[1 - half], normed.at[1, 1 - half], other, "n", "n1"),
        0: send(to_core.at[half], normed.at[1, half], other, "n", "n0"),
    }

    def tokens_of(t, k, far):
        return normed[t, 1 - half if far else half, (y + k) % N_Y]

    def grad_block(k, far):
        return sum(
            lax.dot_general(
                tokens_of(t, k, far), d[t], (((0,), (0,)), ((), ())), preferred_element_type=F32
            )
            for t in range(2)
        )

    mine = pl.ds(pl.multiple_of(bit * mid, mid), mid)
    theirs = pl.ds(pl.multiple_of((1 - bit) * mid, mid), mid)
    first, own = {}, {}

    def send_side(far, way, part_of):
        src = side_out.at[far, way, part_of]
        if along_x:
            ends = ((up, down)[way], (pair_up, pair_down)[way])
            for i, span in enumerate((mine, theirs)):
                dst = side_in.at[far, way, part_of, pl.ds(i * mid, mid)]
                send(src.at[span], dst, ends[i], "side", f"side{far}")
        else:
            send(src, side_in.at[far, way, part_of], (up, down)[way], "side", f"side{far}")

    def reduce_first(far):
        block = grad_block(2, far).astype(BF16)
        first_out[far, 0] = block[:, :cols]
        first_out[far, 1] = block[:, cols:]
        first[far] = [
            send(first_out.at[far, 0], first_in.at[far, 0], up, "first", f"first{far}0"),
            send(first_out.at[far, 1], first_in.at[far, 1], down, "first", f"first{far}1"),
        ]
        for way, k in ((0, 1), (1, 3)):
            block = grad_block(k, far)
            parts = (block[:, :cols], block[:, cols:])
            side_out[far, way, 1 - way] = parts[1 - way].astype(BF16)
            send_side(far, way, 1 - way)
            keep_side[far, way] = parts[way]
        block = grad_block(0, far)
        if not far:
            block = block + 0.9 * mom[...]
        keep[far] = block
        if along_x:
            own_out[far] = keep[far, theirs].astype(BF16)
            own[far] = send(own_out.at[far], own_in.at[far], pair, "own", f"own{far}")

    def reduce_second(far):
        for way in range(2):
            first[far][way].wait_recv()
            side_out[far, way, way] = (
                keep_side[far, way] + first_in[far, way].astype(F32)
            ).astype(BF16)
            send_side(far, way, way)

    def reduced(far, span, copies):
        total = keep[far, span]
        for at_row in copies:
            for way in range(2):
                total = total + jnp.concatenate(
                    [side_in[far, way, c, pl.ds(at_row, mid)] for c in range(2)], axis=1
                ).astype(F32)
        return total

    def wait_reduced(far):
        landed(f"side{far}", side_in.at[far])
        if along_x:
            own[far].wait_recv()

    def project(k, far, begin=False, tokens=(0, 1)):
        for t in tokens:
            new = jnp.dot(tokens_of(t, k, far), wts[4 * far + k], preferred_element_type=F32)
            part[t] = new if begin else part[t] + new

    def back_rows(i):
        n = mid // BACK
        return pl.ds(i * n, n)

    core_d.wait_recv()
    core_n[1].wait_recv()
    reduce_first(1)
    core_n[0].wait_recv()
    load_w.wait()
    load_mom.wait()
    project(0, 0, True)
    reduce_second(1)
    reduce_first(0)


    def start_lower():
        pl.semaphore_wait(ready, len(far_friends))
        start_w()

    pl.when(jnp.logical_not(knows))(start_lower)
    wait_reduced(1)
    if along_x:
        z_out[0] = (reduced(1, mine, (0, mid)) + own_in[1].astype(F32)).astype(BF16)
        for i in range(BACK):
            send(z_out.at[0, back_rows(i)], z_in.at[0, back_rows(i)], across, "z", f"z{i}")
    else:
        for i, span in enumerate((mine, theirs)):
            start = bit * mid if i == 0 else (1 - bit) * mid
            z_out[i] = reduced(1, span, (pl.multiple_of(start, mid),)).astype(BF16)
        for q in range(BACK):
            for i, device in enumerate((across, pair_across)):
                send(z_out.at[i, back_rows(q)], z_in.at[i, back_rows(q)], device, "z", f"z{q}")

    far_up, far_down = {}, {}

    def spread(q):
        w_cross[q].wait_recv()
        s = piece(q)
        for way in (q % 2, 1 - q % 2):
            if way == 0:
                land = f"far{q}" if q % 2 == 0 else "far"
                far_up[q] = send(wts.at[4, s], wts.at[7, s], up, "far", land)
            else:
                land = f"far{q}" if q % 2 else "far"
                far_down[q] = send(wts.at[4, s], wts.at[5, s], down, "far", land)

    def relay(q):
        s = piece(q)
        if q % 2 == 0:
            far_up[q].wait_recv()
            send(wts.at[7, s], wts.at[6, s], up, "far_relay", "far_relay")
        else:
            far_down[q].wait_recv()
            send(wts.at[5, s], wts.at[6, s], down, "far_relay", "far_relay")

    spread(0)
    reduce_second(0)
    if not along_x:
        send_near()
    spread(1)
    relay(0)
    wait_reduced(0)
    if along_x:
        keep[0, mine] = reduced(0, mine, (0, mid)) + own_in[0].astype(F32)
    else:
        z_out[2] = reduced(0, theirs, (pl.multiple_of((1 - bit) * mid, mid),)).astype(BF16)
        for q in range(BACK):
            send(z_out.at[2, back_rows(q)], z_in.at[2, back_rows(q)], pair, "z", f"z{q}")
        keep[0, mine] = reduced(0, mine, (pl.multiple_of(bit * mid, mid),))
    landed("near0", wts.at[1])
    send(wts.at[3, lower], wts.at[2, lower], up, "near_relay", "near_relay")
    send(wts.at[1, upper], wts.at[2, upper], down, "near_relay", "near_relay")
    spread(2)
    relay(1)
    landed("near1", wts.at[1])
    project(1, 0)
    project(3, 0)
    spread(3)
    relay(2)
    project(0, 1)
    relay(3)
    landed("near_relay", wts.at[2])
    project(2, 0)
    landed("far", wts.at[5])
    project(1, 1)
    project(3, 1)

    def finish(q):
        s = back_rows(q)
        n = mid // BACK
        total = keep[0, pl.ds(pl.multiple_of(bit * mid + q * n, n), n)]
        if along_x:
            landed(f"z{q}", z_in.at[0, s])
            total = total + z_in[0, s].astype(F32)
        else:
            landed(f"z{q}", z_in.at[:, s])
            total = total + z_in[0, s].astype(F32) + z_in[1, s].astype(F32) + z_in[2, s].astype(F32)
        result = 0.5 * total
        back_out[s] = result.astype(BF16)
        send(back_out.at[s], back_in.at[s], pair, "back", "back")
        averaged_ref[pl.ds(pl.multiple_of(bit * mid + q * n, n), n)] = result

    for q in range(BACK):
        finish(q)
    landed("far_relay", wts.at[6])
    project(2, 1, tokens=(1,))
    vals_send = send(part.at[1], vals_in, other, "vals", "vals")
    project(2, 1, tokens=(0,))
    vals_send.wait_recv()
    values_ref[...] = (part[0] + vals_in[...]).astype(BF16)
    landed("back", back_in)
    averaged_ref[theirs] = back_in[...].astype(F32)

    total_of = {
        "w": wts.at[4],
        "d": d.at[0],
        "n": to_core,
        "first": first_out,
        "side": side_out,
        "own": own_out,
        "z": z_out.at[0] if along_x else z_out,
        "far": wts.at[pl.ds(4, 2)],
        "far_relay": wts.at[6],
        "near": wts.at[pl.ds(0, 2)],
        "near_relay": wts.at[2],
        "vals": vals_in,
        "back": back_in,
    }
    assert len(leaving) <= N_SEND and len(landing) <= N_RECV
    for leave, i in leaving.items():
        pltpu.make_async_copy(total_of[leave], total_of[leave], send_sem.at[i]).wait()


def fused(level, hidden, gain, weight, cotangent, momentum):
    rows, feats = hidden.shape
    blk, kv = weight.shape
    mid, cols = blk // 2, kv // 2
    anywhere = pl.BlockSpec(memory_space=pl.ANY)
    vmem = pl.BlockSpec(memory_space=pltpu.VMEM)
    return pl.pallas_call(
        partial(kernel, level),
        name=f"layer_level_{level}",
        out_shape=(
            jax.ShapeDtypeStruct((rows, kv), BF16),
            jax.ShapeDtypeStruct((blk, kv), F32),
        ),
        in_specs=[anywhere, vmem, anywhere, anywhere, anywhere],
        out_specs=(vmem, vmem),
        scratch_shapes=[
            pltpu.VMEM((rows, feats), BF16),
            pltpu.VMEM((blk, kv), F32),
            pltpu.VMEM((2, 2, N_Y, rows, blk), BF16),
            pltpu.VMEM((2, N_Y, rows, blk), BF16),
            pltpu.VMEM((2, rows, kv), BF16),
            pltpu.VMEM((2 * N_Y, blk, kv), BF16),
            pltpu.VMEM((2, rows, kv), F32),
            pltpu.VMEM((rows, kv), F32),
            pltpu.VMEM((2, blk, kv), F32),
            pltpu.VMEM((2, 2, blk, cols), F32),
            pltpu.VMEM((2, 2, blk, cols), BF16),
            pltpu.VMEM((2, 2, blk, cols), BF16),
            pltpu.VMEM((2, 2, 2, blk, cols), BF16),
            pltpu.VMEM((2, 2, 2, blk, cols), BF16),
            pltpu.VMEM((2, mid, kv), BF16),
            pltpu.VMEM((2, mid, kv), BF16),
            pltpu.VMEM((3, mid, kv), BF16),
            pltpu.VMEM((3, mid, kv), BF16),
            pltpu.VMEM((mid, kv), BF16),
            pltpu.VMEM((mid, kv), BF16),
            pltpu.SemaphoreType.DMA((4,)),
            pltpu.SemaphoreType.DMA((N_SEND,)),
            pltpu.SemaphoreType.DMA((N_RECV,)),
            pltpu.SemaphoreType.REGULAR,
        ],
        compiler_params=pltpu.CompilerParams(
            collective_id=level, has_side_effects=True, vmem_limit_bytes=40 << 20
        ),
    )(hidden, gain, weight, cotangent, momentum)


def store_kernel(values_ref, averaged_ref, values_out, averaged_out, sems):
    copies = [
        pltpu.make_async_copy(values_ref, values_out, sems.at[0]),
        pltpu.make_async_copy(averaged_ref, averaged_out, sems.at[1]),
    ]
    for copy in copies:
        copy.start()
    for copy in copies:
        copy.wait()


def store(values, averaged):
    anywhere = pl.BlockSpec(memory_space=pl.ANY)
    return pl.pallas_call(
        store_kernel,
        name="store",
        out_shape=(
            jax.ShapeDtypeStruct(values.shape, values.dtype),
            jax.ShapeDtypeStruct(averaged.shape, averaged.dtype),
        ),
        in_specs=[anywhere, anywhere],
        out_specs=(anywhere, anywhere),
        scratch_shapes=[pltpu.SemaphoreType.DMA((2,))],
    )(values, averaged)


def local(hidden_in, norm_gain, w_value, d_values, momentum, step):
    levels = lax.axis_size("rep").bit_length() - 1
    branches = [partial(fused, level) for level in range(levels)]
    values, averaged = lax.switch(
        lax.rem(step, levels), branches, hidden_in[0], norm_gain, w_value[0], d_values[0], momentum[0]
    )
    values, averaged = store(values, averaged)
    return (values[None], averaged[None])


def solution(mesh):
    placed = (
        P("rep", "fsdp", None),
        P("rep", None),
        P("rep", "fsdp", None),
        P("rep", "fsdp", None),
        P("rep", "fsdp", None),
        P(),
    )
    return jax.shard_map(
        local,
        mesh=mesh,
        in_specs=placed,
        out_specs=(P("rep", "fsdp", None), P("rep", "fsdp", None)),
        check_vma=False,
    )
```
